32 devices in a mesh: space: 16 (over z, x, core), rep: 2 (over y).
Axes of the slice: x: 2, y: 2, z: 4, core: 2. Of those that a mesh axis runs over, the one named last changes fastest.
Arguments:
- input_field: bfloat16 [2, 128, 128, 32, 128], P('rep', 'space'), may hold values from -6 to 6
- cotangent: bfloat16 [2, 128, 128, 32, 128], P('rep', 'space'), may hold values from -6 to 6
- mode_weight: float32 [256, 24, 2048], P('space', 'rep'), may hold values from -0.004 to 0.004
- first_moment: float32 [256, 24, 2048], P('space', 'rep'), may hold values from -3 to 3
- second_moment: float32 [256, 24, 2048], P('space', 'rep'), may hold values from 0.001 to 0.05
Outputs:
- layer_output: bfloat16 [2, 128, 128, 32, 128], P('rep', 'space')
- input_gradient: bfloat16 [2, 128, 128, 32, 128], P('rep', 'space')
- new_weight: float32 [256, 24, 2048], P('space', 'rep')
- new_first: float32 [256, 24, 2048], P('space', 'rep')
- new_second: float32 [256, 24, 2048], P('space', 'rep')
The draws below stay inside these ranges and needn't reach their ends.
All inputs are finite; a program needn't handle non-finite values.
Results may differ from the reference program's by a relative error of at most 0.019.
Values may be sent and summed in bfloat16 or wider, within the bound.
A program may use at most 128 MiB of HBM per device.

```python
import math
import jax
import jax.numpy as jnp
from jax import lax

C = 32
NX = 128
NY = 128
NZ = 128
KX = 24
KY = 16
KZ = 16
STEP = 10
SAMPLES = 2


def level_of(key, shape, pieces, least, high):
    def one(axis_at, blocks):
        draws = jax.random.uniform(jax.random.fold_in(jax.random.fold_in(key, 6), axis_at), (blocks,), jnp.float32, least / len(pieces), high / len(pieces))
        return jnp.repeat(jnp.exp(draws), shape[axis_at] // blocks).reshape((-1,) + (1,) * (len(shape) - axis_at - 1))

    factor_of = one(*pieces[0])
    for cut in pieces[1:]:
        factor_of = factor_of * one(*cut)
    return factor_of


def normal_values(rng, shape, spread, bound, cuts=(), kind=jnp.bfloat16):
    values = jax.random.normal(rng, shape, jnp.float32) * spread
    if len(cuts) > 0:
        values = level_of(rng, shape, cuts, -0.22, 0.18) * values
    return jnp.clip(values, min=-bound, max=bound).astype(kind)


def setup_inputs(seed: int = 0) -> dict:
    key_list = jax.random.split(jax.random.key(seed), 6)
    input_field = normal_values(key_list[0], (SAMPLES, NX, NY, C, NZ), 1.0, 6.0, ((0, 2), (1, 16)))
    cotangent = normal_values(key_list[1], (SAMPLES, NX, NY, C, NZ), 1.0, 6.0, ((0, 2), (1, 16)))
    mode_weight = jnp.clip(jax.random.uniform(key_list[2], (KY * KZ, KX, 2 * C * C), jnp.float32, -0.004, 0.004) * level_of(key_list[2], (KY * KZ, KX, 2 * C * C), ((0, 16), (1, 2)), -0.4, 0.0), -0.004, 0.004)
    first_moment = normal_values(key_list[3], (KY * KZ, KX, 2 * C * C), 0.5, 3.0, ((0, 16), (1, 2)), jnp.float32)
    second_moment = jnp.clip(jnp.exp(math.log(0.05) - 3.912023 * jax.random.uniform(key_list[4], (KY * KZ, KX, 2 * C * C), jnp.float32) ** level_of(key_list[4], (KY * KZ, KX, 2 * C * C), ((0, 16), (1, 2)), -0.2, 0.2)), 0.001, 0.05)
    return dict(input_field=input_field, cotangent=cotangent, mode_weight=mode_weight, first_moment=first_moment, second_moment=second_moment)


beta_one = 0.9
beta_two = 0.999
learning_rate = 0.001
epsilon = 1e-08

def kept_frequency(count, length):
    number = jnp.arange(count, dtype=jnp.int32)
    return jnp.where(number < count // 2, number, length - count + number).astype(jnp.int32)

def wave_tables(frequency, length):
    position = jnp.arange(length, dtype=jnp.int32)
    product = frequency[:, None] * position[None, :] % length
    radians = product.astype(jnp.float32) * (2.0 * math.pi / length)
    return (jnp.cos(radians), jnp.sin(radians))

def build_tables():
    plane_cosine, plane_sine = wave_tables(kept_frequency(KX, NX), NX)
    row_cosine, row_sine = wave_tables(kept_frequency(KY, NY), NY)
    depth_cosine, depth_sine = wave_tables(jnp.arange(KZ, dtype=jnp.int32), NZ)
    weighting = jnp.where(jnp.arange(KZ) == 0, 1.0, 2.0).astype(jnp.float32)
    doubled = jnp.concatenate([weighting, weighting])
    depth_forward = jnp.concatenate([depth_cosine.T, -depth_sine.T], axis=1)
    depth_inverse = jnp.concatenate([depth_cosine, -depth_sine], axis=0)
    field_table = depth_forward.astype(jnp.bfloat16)
    grad_table = (depth_forward * doubled[None, :]).astype(jnp.bfloat16)
    output_table = (depth_inverse * doubled[:, None]).astype(jnp.bfloat16)
    plain_table = depth_inverse.astype(jnp.bfloat16)
    return (plane_cosine.astype(jnp.bfloat16), plane_sine.astype(jnp.bfloat16), row_cosine.astype(jnp.bfloat16), row_sine.astype(jnp.bfloat16), field_table, grad_table, output_table, plain_table)

def plane_modes(grid, depth_table, row_cosine, row_sine):
    samples, planes = (grid.shape[0], grid.shape[1])
    depth = jnp.dot(grid, depth_table, preferred_element_type=jnp.float32).astype(jnp.bfloat16)
    depth = depth.reshape(samples, planes, NY, C, 2, KZ).astype(jnp.float32)
    cosine_part = jnp.einsum('qy,bxycrs->bxrcqs', row_cosine.astype(jnp.float32), depth)
    sine_part = jnp.einsum('qy,bxycrs->bxrcqs', row_sine.astype(jnp.float32), depth)
    real_part = cosine_part[:, :, 0] + sine_part[:, :, 1]
    imag_part = cosine_part[:, :, 1] - sine_part[:, :, 0]
    stacked = jnp.stack([real_part, imag_part], axis=2)
    return stacked.reshape(samples, planes, 2, C, KY * KZ).astype(jnp.bfloat16)

def grid_modes(columns, plane_cosine, plane_sine, norm_scale):
    values = columns.astype(jnp.float32)
    cosine_part = jnp.einsum('kx,bxrcm->bkrcm', plane_cosine.astype(jnp.float32), values)
    sine_part = jnp.einsum('kx,bxrcm->bkrcm', plane_sine.astype(jnp.float32), values)
    real_part = cosine_part[:, :, 0] + sine_part[:, :, 1]
    imag_part = cosine_part[:, :, 1] - sine_part[:, :, 0]
    return (jnp.stack([real_part, imag_part], axis=2) * norm_scale).astype(jnp.bfloat16)

def mix_modes(modes, mixer):
    product = jnp.einsum('bkrcm,mksco->bkrsom', modes.astype(jnp.float32), mixer.astype(jnp.float32))
    real_part = product[:, :, 0, 0] - product[:, :, 1, 1]
    imag_part = product[:, :, 0, 1] + product[:, :, 1, 0]
    return jnp.stack([real_part, imag_part], axis=2).astype(jnp.bfloat16)

def back_modes(grads, mixer):
    product = jnp.einsum('bkrom,mksco->bkrscm', grads.astype(jnp.float32), mixer.astype(jnp.float32))
    real_part = product[:, :, 0, 0] + product[:, :, 1, 1]
    imag_part = product[:, :, 1, 0] - product[:, :, 0, 1]
    return jnp.stack([real_part, imag_part], axis=2).astype(jnp.bfloat16)

def weight_gradient(modes, grads):
    product = jnp.einsum('bkrcm,bksom->mkrsco', modes.astype(jnp.float32), grads.astype(jnp.float32))
    real_part = product[:, :, 0, 0] + product[:, :, 1, 1]
    imag_part = product[:, :, 0, 1] - product[:, :, 1, 0]
    stacked = jnp.stack([real_part, imag_part], axis=2)
    return stacked.reshape(stacked.shape[0], stacked.shape[1], 2 * C * C)

def mode_planes(modes, plane_cosine, plane_sine):
    values = modes.astype(jnp.float32)
    cosine_part = jnp.einsum('kx,bkrcm->bxrcm', plane_cosine.astype(jnp.float32), values)
    sine_part = jnp.einsum('kx,bkrcm->bxrcm', plane_sine.astype(jnp.float32), values)
    real_part = cosine_part[:, :, 0] - sine_part[:, :, 1]
    imag_part = cosine_part[:, :, 1] + sine_part[:, :, 0]
    return jnp.stack([real_part, imag_part], axis=2).astype(jnp.bfloat16)

def plane_grid(columns, row_cosine, row_sine, depth_table, norm_scale):
    samples, planes = (columns.shape[0], columns.shape[1])
    values = columns.reshape(samples, planes, 2, C, KY, KZ).astype(jnp.float32)
    cosine_part = jnp.einsum('qy,bxrcqs->bxycrs', row_cosine.astype(jnp.float32), values)
    sine_part = jnp.einsum('qy,bxrcqs->bxycrs', row_sine.astype(jnp.float32), values)
    real_part = cosine_part[:, :, :, :, 0] - sine_part[:, :, :, :, 1]
    imag_part = cosine_part[:, :, :, :, 1] + sine_part[:, :, :, :, 0]
    rows = jnp.stack([real_part, imag_part], axis=4).reshape(samples, planes, NY, C, 2 * KZ).astype(jnp.bfloat16)
    result = jnp.dot(rows, depth_table, preferred_element_type=jnp.float32) * norm_scale
    return result.astype(jnp.bfloat16)

def reference(input_field, cotangent, mode_weight, first_moment, second_moment):
    plane_cosine, plane_sine, row_cosine, row_sine, field_table, grad_table, output_table, plain_table = build_tables()
    norm_scale = 1.0 / math.sqrt(NX * NY * NZ)
    mixer = mode_weight.astype(jnp.bfloat16).reshape(KY * KZ, KX, 2, C, C)

    def one_sample(total, pair):
        grid = pair[0][None]
        grad = pair[1][None]
        field_modes = grid_modes(plane_modes(grid, field_table, row_cosine, row_sine), plane_cosine, plane_sine, norm_scale)
        grad_modes = grid_modes(plane_modes(grad, grad_table, row_cosine, row_sine), plane_cosine, plane_sine, norm_scale)
        mixed = mode_planes(mix_modes(field_modes, mixer), plane_cosine, plane_sine)
        output = plane_grid(mixed, row_cosine, row_sine, output_table, norm_scale)
        backed = mode_planes(back_modes(grad_modes, mixer), plane_cosine, plane_sine)
        in_grad = plane_grid(backed, row_cosine, row_sine, plain_table, norm_scale)
        return (total + weight_gradient(field_modes, grad_modes), (output[0], in_grad[0]))
    start = jnp.zeros((KY * KZ, KX, 2 * C * C), jnp.float32)
    gradient, (layer_output, input_gradient) = lax.scan(one_sample, start, (input_field, cotangent))
    new_first = beta_one * first_moment + (1.0 - beta_one) * gradient
    new_second = beta_two * second_moment + (1.0 - beta_two) * gradient * gradient
    corrected = new_first / (1.0 - beta_one ** STEP) / (jnp.sqrt(new_second / (1.0 - beta_two ** STEP)) + epsilon)
    new_weight = mode_weight - learning_rate * corrected
    return (layer_output, input_gradient, new_weight, new_first, new_second)
```

```python
import functools
import math

import jax
import jax.numpy as jnp
import numpy as np
from jax import lax
from jax.experimental import pallas as pl
from jax.experimental.pallas import tpu as pltpu
from jax.sharding import PartitionSpec as P

C = 32
NX = 128
NY = 128
NZ = 128
KX = 24
KY = 16
KZ = 16
STEP = 10
CC = C * C
LANES = 4 * C
ROWS = 16

beta_one = 0.9
beta_two = 0.999
learning_rate = 0.001
epsilon = 1e-08
norm_scale = 1.0 / math.sqrt(NX * NY * NZ)

f32 = jnp.float32
bf16 = jnp.bfloat16


def kept_frequency(count, length):
    number = np.arange(count)
    return np.where(number < count // 2, number, length - count + number)


def wave_tables(frequency, length):
    product = frequency[:, None] * np.arange(length)[None, :] % length
    radians = product * (2.0 * math.pi / length)
    return np.cos(radians).astype(np.float32), np.sin(radians).astype(np.float32)


def constant(array):
    return jnp.asarray(np.asarray(array, np.float32), dtype=bf16)


def depth_tables():
    cosine, sine = wave_tables(np.arange(KZ), NZ)
    weighting = np.where(np.arange(KZ) == 0, 1.0, 2.0)[:, None]
    plain = np.concatenate([cosine, -sine], axis=0)
    doubled = np.concatenate([weighting * cosine, -weighting * sine], axis=0)
    return constant(plain), constant(doubled)


def row_table():
    cosine, sine = wave_tables(kept_frequency(KY, NY), NY)
    return constant(np.stack([np.stack([cosine, sine]), np.stack([-sine, cosine])]))


def plane_table(reps):
    own = KX // reps
    cosine, sine = wave_tables(kept_frequency(KX, NX), NX)
    tables = np.zeros((2, reps, ROWS, NX), np.float32)
    tables[0, :, :own] = cosine.reshape(reps, own, NX)
    tables[1, :, :own] = sine.reshape(reps, own, NX)
    return tables.reshape(2, reps * ROWS, NX)


def rotation():
    table = np.zeros((LANES, LANES), np.float32)
    for field in range(2):
        for c in range(C):
            real, imag = field * 2 * C + c, field * 2 * C + C + c
            table[imag, real] = 1.0
            table[real, imag] = -1.0
    return constant(table)


def spread_tables():
    table = np.zeros((LANES, 4, CC), np.float32)
    pair = np.arange(CC)
    for part in range(2):
        table[part * C + pair // C, part, pair] = 1.0
        table[2 * C + part * C + pair % C, 2 + part, pair] = 1.0
    return constant(table.reshape(LANES, 4 * CC))


def gather_tables():
    table = np.zeros((4, CC, LANES), np.float32)
    pair = np.arange(CC)
    for part in range(2):
        table[part, pair, part * C + pair % C] = 1.0
        table[2 + part, pair, 2 * C + part * C + pair // C] = 1.0
    return constant(table)


def depth_kernel(field_ref, grad_ref, field_table, grad_table, out_ref):
    for k, (ref, table) in enumerate(((field_ref, field_table), (grad_ref, grad_table))):
        out_ref[k, 0] = lax.dot_general(
            table[...], ref[0], (((1,), (1,)), ((), ())), preferred_element_type=f32
        ).astype(bf16)


def depth_forward(input_field, cotangent):
    plain, doubled = depth_tables()
    planes = input_field.shape[1]
    rows = NY * C
    block = pl.BlockSpec((1, rows, NZ), lambda i: (i, 0, 0))
    table = pl.BlockSpec((2 * KZ, NZ), lambda i: (0, 0))
    return pl.pallas_call(
        depth_kernel,
        grid=(planes,),
        in_specs=[block, block, table, table],
        out_specs=pl.BlockSpec((2, 1, 2 * KZ, rows), lambda i: (0, i, 0, 0)),
        out_shape=jax.ShapeDtypeStruct((2, planes, 2 * KZ, rows), bf16),
        compiler_params=pltpu.CompilerParams(vmem_limit_bytes=40 * 2**20),
        name="depth_forward",
    )(input_field.reshape(planes, rows, NZ), cotangent.reshape(planes, rows, NZ), plain, doubled)


def grid_kernel(rows_ref, output_table, grad_table, output_ref, grad_ref):
    for k, (ref, table) in enumerate(((output_ref, output_table), (grad_ref, grad_table))):
        ref[0] = (
            lax.dot_general(
                rows_ref[k, 0], table[...], (((0,), (0,)), ((), ())), preferred_element_type=f32
            )
            * norm_scale
        ).astype(bf16)


def depth_inverse(rows_in):
    plain, doubled = depth_tables()
    planes, rows = rows_in.shape[1], NY * C
    block = pl.BlockSpec((1, rows, NZ), lambda i: (i, 0, 0))
    table = pl.BlockSpec((2 * KZ, NZ), lambda i: (0, 0))
    outputs = pl.pallas_call(
        grid_kernel,
        grid=(planes,),
        in_specs=[pl.BlockSpec((2, 1, 2 * KZ, rows), lambda i: (0, i, 0, 0)), table, table],
        out_specs=[block, block],
        out_shape=[jax.ShapeDtypeStruct((planes, rows, NZ), bf16)] * 2,
        compiler_params=pltpu.CompilerParams(vmem_limit_bytes=40 * 2**20),
        name="depth_inverse",
    )(rows_in, doubled, plain)
    return [value.reshape(1, planes, NY, C, NZ) for value in outputs]


def modes_kernel(reps, columns_ref, table_ref, turn_ref, out_ref):
    for m in range(columns_ref.shape[0]):
        columns = columns_ref[m]
        turned = jnp.dot(columns, turn_ref[...], preferred_element_type=f32).astype(bf16)
        both = jnp.concatenate([columns, turned], axis=0)
        modes = jnp.dot(table_ref[...], both, preferred_element_type=f32) * norm_scale
        modes = modes.astype(bf16)
        for r in range(reps):
            out_ref[r, m] = modes[r * ROWS : (r + 1) * ROWS]


def grid_modes(columns, reps):
    cosine, sine = plane_table(reps)
    owned = columns.shape[0]
    return pl.pallas_call(
        functools.partial(modes_kernel, reps),
        out_shape=jax.ShapeDtypeStruct((reps, owned, ROWS, LANES), bf16),
        compiler_params=pltpu.CompilerParams(vmem_limit_bytes=40 * 2**20),
        name="grid_modes",
    )(columns, constant(np.concatenate([cosine, sine], axis=1)), rotation())


def planes_kernel(reps, modes_ref, table_ref, turn_ref, out_ref):
    for m in range(out_ref.shape[0]):
        modes = jnp.concatenate([modes_ref[r, m] for r in range(reps)], axis=0)
        turned = jnp.dot(modes, turn_ref[...], preferred_element_type=f32).astype(bf16)
        both = jnp.concatenate([modes, turned], axis=0)
        out_ref[m] = jnp.dot(table_ref[...], both, preferred_element_type=f32).astype(bf16)


def mode_planes(modes, reps):
    cosine, sine = plane_table(reps)
    owned = modes.shape[1]
    return pl.pallas_call(
        functools.partial(planes_kernel, reps),
        out_shape=jax.ShapeDtypeStruct((owned, NX, LANES), bf16),
        compiler_params=pltpu.CompilerParams(vmem_limit_bytes=40 * 2**20),
        name="mode_planes",
    )(modes, constant(np.concatenate([cosine.T, -sine.T], axis=1)), rotation())


def mix_kernel(
    modes_ref, weight_ref, first_ref, second_ref, spread_ref, gather_ref,
    mixed_ref, new_weight_ref, new_first_ref, new_second_ref, padded,
):
    samples, owned = modes_ref.shape[0], modes_ref.shape[1]
    own = weight_ref.shape[1]
    rows = owned * ROWS
    padded[...] = jnp.zeros_like(padded)
    padded[:, :own] = weight_ref[...].astype(bf16).astype(f32)
    weight = padded[...].reshape(rows, 2 * CC)
    real, imag = weight[:, :CC], weight[:, CC:]
    grad_real = jnp.zeros((rows, CC), f32)
    grad_imag = jnp.zeros((rows, CC), f32)
    for b in range(samples):
        modes = modes_ref[b].reshape(rows, LANES)
        ur, ui, gr, gi = [
            jnp.dot(modes, spread_ref[:, k * CC : (k + 1) * CC], preferred_element_type=f32)
            for k in range(4)
        ]
        terms = (
            ur * real - ui * imag,
            ur * imag + ui * real,
            gr * real + gi * imag,
            gi * real - gr * imag,
        )
        mixed = jnp.zeros((rows, LANES), f32)
        for k in range(4):
            mixed += jnp.dot(terms[k].astype(bf16), gather_ref[k], preferred_element_type=f32)
        mixed_ref[b] = mixed.astype(bf16).reshape(owned, ROWS, LANES)
        grad_real += ur * gr + ui * gi
        grad_imag += ur * gi - ui * gr
    for part, gradient in enumerate((grad_real, grad_imag)):
        lanes = slice(part * CC, (part + 1) * CC)
        gradient = gradient.reshape(owned, ROWS, CC)[:, :own]
        new_first = beta_one * first_ref[:, :, lanes] + (1.0 - beta_one) * gradient
        new_second = (
            beta_two * second_ref[:, :, lanes] + (1.0 - beta_two) * gradient * gradient
        )
        corrected = (new_first / (1.0 - beta_one**STEP)) / (
            jnp.sqrt(new_second / (1.0 - beta_two**STEP)) + epsilon
        )
        new_first_ref[:, :, lanes] = new_first
        new_second_ref[:, :, lanes] = new_second
        new_weight_ref[:, :, lanes] = weight_ref[:, :, lanes] - learning_rate * corrected


def mix_and_update(modes, mode_weight, first_moment, second_moment):
    samples, owned = modes.shape[0], modes.shape[1]
    own = mode_weight.shape[1]
    step = min(owned, 4)
    weights = pl.BlockSpec((step, own, 2 * CC), lambda i: (i, 0, 0))
    blocks = pl.BlockSpec((samples, step, ROWS, LANES), lambda i: (0, i, 0, 0))
    like_weight = jax.ShapeDtypeStruct(mode_weight.shape, f32)
    return pl.pallas_call(
        mix_kernel,
        grid=(owned // step,),
        in_specs=[
            blocks,
            weights,
            weights,
            weights,
            pl.BlockSpec((LANES, 4 * CC), lambda i: (0, 0)),
            pl.BlockSpec((4, CC, LANES), lambda i: (0, 0, 0)),
        ],
        out_specs=[blocks, weights, weights, weights],
        out_shape=[jax.ShapeDtypeStruct(modes.shape, bf16), like_weight, like_weight, like_weight],
        scratch_shapes=[pltpu.VMEM((step, ROWS, 2 * CC), f32)],
        compiler_params=pltpu.CompilerParams(vmem_limit_bytes=48 * 2**20),
        name="mix_and_update",
    )(modes, mode_weight, first_moment, second_moment, spread_tables(), gather_tables())


def local(reps, input_field, cotangent, mode_weight, first_moment, second_moment):
    planes = input_field.shape[1]
    rows = row_table()
    depth = depth_forward(input_field, cotangent)
    depth = depth.reshape(2, planes, 2, KZ, NY, C)
    slabs = jnp.einsum("rpqy,fxpsyc->qsxfrc", rows, depth, preferred_element_type=f32)
    slabs = slabs.astype(bf16).reshape(KY * KZ, planes, LANES)
    columns = lax.all_to_all(slabs, "space", split_axis=0, concat_axis=1, tiled=True)
    modes = grid_modes(columns, reps)
    modes = lax.all_to_all(modes, "rep", split_axis=0, concat_axis=0, tiled=True)
    mixed, new_weight, new_first, new_second = mix_and_update(
        modes, mode_weight, first_moment, second_moment
    )
    mixed = lax.all_to_all(mixed, "rep", split_axis=0, concat_axis=0, tiled=True)
    columns = mode_planes(mixed, reps)
    slabs = lax.all_to_all(columns, "space", split_axis=1, concat_axis=0, tiled=True)
    slabs = slabs.reshape(KY, KZ, planes, 2, 2, C)
    grid_rows = jnp.einsum("rpqy,qsxfrc->fxpsyc", rows, slabs, preferred_element_type=f32)
    grid_rows = grid_rows.astype(bf16).reshape(2, planes, 2 * KZ, NY * C)
    layer_output, input_gradient = depth_inverse(grid_rows)
    return (layer_output, input_gradient, new_weight, new_first, new_second)


def solution(mesh):
    grids = P("rep", "space", None, None, None)
    weights = P("space", "rep", None)
    return jax.shard_map(
        functools.partial(local, mesh.shape["rep"]),
        mesh=mesh,
        in_specs=(grids, grids, weights, weights, weights),
        out_specs=(grids, grids, weights, weights, weights),
        check_vma=False,
    )
```

```python
import functools
import math

import jax
import jax.numpy as jnp
import numpy as np
from jax import lax
from jax.experimental import pallas as pl
from jax.experimental.pallas import tpu as pltpu
from jax.sharding import PartitionSpec as P

C = 32
NX = 128
NY = 128
NZ = 128
KX = 24
KY = 16
KZ = 16
STEP = 10
CC = C * C
LANES = 4 * C
ROWS = 16

beta_one = 0.9
beta_two = 0.999
learning_rate = 0.001
epsilon = 1e-08
norm_scale = 1.0 / math.sqrt(NX * NY * NZ)

f32 = jnp.float32
bf16 = jnp.bfloat16


def kept_frequency(count, length):
    number = np.arange(count)
    return np.where(number < count // 2, number, length - count + number)


def wave_tables(frequency, length):
    product = frequency[:, None] * np.arange(length)[None, :] % length
    radians = product * (2.0 * math.pi / length)
    return np.cos(radians).astype(np.float32), np.sin(radians).astype(np.float32)


def constant(array):
    return jnp.asarray(np.asarray(array, np.float32), dtype=bf16)


def depth_tables():
    cosine, sine = wave_tables(np.arange(KZ), NZ)
    weighting = np.where(np.arange(KZ) == 0, 1.0, 2.0)[:, None]
    plain = np.concatenate([cosine, -sine], axis=0)
    doubled = np.concatenate([weighting * cosine, -weighting * sine], axis=0)
    return constant(plain), constant(doubled)


def row_tables():
    cosine, sine = wave_tables(kept_frequency(KY, NY), NY)
    return constant(cosine), constant(sine)


def plane_table(reps):
    own = KX // reps
    cosine, sine = wave_tables(kept_frequency(KX, NX), NX)
    tables = np.zeros((2, reps, ROWS, NX), np.float32)
    tables[0, :, :own] = cosine.reshape(reps, own, NX)
    tables[1, :, :own] = sine.reshape(reps, own, NX)
    return tables.reshape(2, reps * ROWS, NX)


def rotation():
    table = np.zeros((LANES, LANES), np.float32)
    for field in range(2):
        for c in range(C):
            real, imag = field * 2 * C + c, field * 2 * C + C + c
            table[imag, real] = 1.0
            table[real, imag] = -1.0
    return constant(table)


def spread_tables():
    table = np.zeros((LANES, 4, CC), np.float32)
    pair = np.arange(CC)
    for part in range(2):
        table[part * C + pair // C, part, pair] = 1.0
        table[2 * C + part * C + pair % C, 2 + part, pair] = 1.0
    return constant(table.reshape(LANES, 4 * CC))


def gather_tables():
    table = np.zeros((4, CC, LANES), np.float32)
    pair = np.arange(CC)
    for part in range(2):
        table[part, pair, part * C + pair % C] = 1.0
        table[2 + part, pair, 2 * C + part * C + pair // C] = 1.0
    return constant(table)


def depth_kernel(field_ref, grad_ref, field_table, grad_table, out_ref):
    out_ref[0] = (
        jnp.dot(field_ref[0], field_table[...], preferred_element_type=f32)
        + jnp.dot(grad_ref[0], grad_table[...], preferred_element_type=f32)
    ).astype(bf16)


def lane_table(table, field):
    real, imag = table[:KZ].T, table[KZ:].T
    own = jnp.concatenate([real, imag], axis=1)
    turned = jnp.concatenate([imag, -real], axis=1)
    none = jnp.zeros_like(own)
    halves = [[half, none] if field == 0 else [none, half] for half in (own, turned)]
    return jnp.concatenate(halves[0] + halves[1], axis=1)


def depth_forward(input_field, cotangent):
    plain, doubled = depth_tables()
    planes = input_field.shape[1]
    rows = NY * C
    block = pl.BlockSpec((1, rows, NZ), lambda i: (i, 0, 0))
    table = pl.BlockSpec((NZ, 8 * KZ), lambda i: (0, 0))
    return pl.pallas_call(
        depth_kernel,
        grid=(planes,),
        in_specs=[block, block, table, table],
        out_specs=pl.BlockSpec((1, rows, 8 * KZ), lambda i: (i, 0, 0)),
        out_shape=jax.ShapeDtypeStruct((planes, rows, 8 * KZ), bf16),
        compiler_params=pltpu.CompilerParams(vmem_limit_bytes=40 * 2**20),
        name="depth_forward",
    )(
        input_field.reshape(planes, rows, NZ),
        cotangent.reshape(planes, rows, NZ),
        lane_table(plain, 0),
        lane_table(doubled, 1),
    )


def grid_kernel(rows_ref, output_table, grad_table, output_ref, grad_ref):
    for ref, table in ((output_ref, output_table), (grad_ref, grad_table)):
        ref[0] = (
            jnp.dot(rows_ref[0], table[...], preferred_element_type=f32) * norm_scale
        ).astype(bf16)


def depth_inverse(rows_in):
    plain, doubled = depth_tables()
    planes, rows = rows_in.shape[0], NY * C
    block = pl.BlockSpec((1, rows, NZ), lambda i: (i, 0, 0))
    table = pl.BlockSpec((8 * KZ, NZ), lambda i: (0, 0))
    outputs = pl.pallas_call(
        grid_kernel,
        grid=(planes,),
        in_specs=[pl.BlockSpec((1, rows, 8 * KZ), lambda i: (i, 0, 0)), table, table],
        out_specs=[block, block],
        out_shape=[jax.ShapeDtypeStruct((planes, rows, NZ), bf16)] * 2,
        compiler_params=pltpu.CompilerParams(vmem_limit_bytes=40 * 2**20),
        name="depth_inverse",
    )(rows_in, lane_table(doubled, 0).T, lane_table(plain, 1).T)
    return [value.reshape(1, planes, NY, C, NZ) for value in outputs]


def modes_kernel(reps, columns_ref, table_ref, turn_ref, out_ref):
    for m in range(columns_ref.shape[0]):
        columns = columns_ref[m]
        turned = jnp.dot(columns, turn_ref[...], preferred_element_type=f32).astype(bf16)
        both = jnp.concatenate([columns, turned], axis=0)
        modes = jnp.dot(table_ref[...], both, preferred_element_type=f32) * norm_scale
        modes = modes.astype(bf16)
        for r in range(reps):
            out_ref[r, m] = modes[r * ROWS : (r + 1) * ROWS]


def grid_modes(columns, reps):
    cosine, sine = plane_table(reps)
    owned = columns.shape[0]
    return pl.pallas_call(
        functools.partial(modes_kernel, reps),
        out_shape=jax.ShapeDtypeStruct((reps, owned, ROWS, LANES), bf16),
        compiler_params=pltpu.CompilerParams(vmem_limit_bytes=40 * 2**20),
        name="grid_modes",
    )(columns, constant(np.concatenate([cosine, sine], axis=1)), rotation())


def planes_kernel(reps, modes_ref, table_ref, turn_ref, out_ref):
    for m in range(out_ref.shape[0]):
        modes = jnp.concatenate([modes_ref[r, m] for r in range(reps)], axis=0)
        turned = jnp.dot(modes, turn_ref[...], preferred_element_type=f32).astype(bf16)
        both = jnp.concatenate([modes, turned], axis=0)
        out_ref[m] = jnp.dot(table_ref[...], both, preferred_element_type=f32).astype(bf16)


def mode_planes(modes, reps):
    cosine, sine = plane_table(reps)
    owned = modes.shape[1]
    return pl.pallas_call(
        functools.partial(planes_kernel, reps),
        out_shape=jax.ShapeDtypeStruct((owned, NX, LANES), bf16),
        compiler_params=pltpu.CompilerParams(vmem_limit_bytes=40 * 2**20),
        name="mode_planes",
    )(modes, constant(np.concatenate([cosine.T, -sine.T], axis=1)), rotation())


def mix_kernel(
    modes_ref, weight_ref, first_ref, second_ref, spread_ref, gather_ref,
    mixed_ref, new_weight_ref, new_first_ref, new_second_ref, padded,
):
    samples, owned = modes_ref.shape[0], modes_ref.shape[1]
    own = weight_ref.shape[1]
    rows = owned * ROWS
    padded[...] = jnp.zeros_like(padded)
    padded[:, :own] = weight_ref[...].astype(bf16).astype(f32)
    weight = padded[...].reshape(rows, 2 * CC)
    real, imag = weight[:, :CC], weight[:, CC:]
    grad_real = jnp.zeros((rows, CC), f32)
    grad_imag = jnp.zeros((rows, CC), f32)
    for b in range(samples):
        modes = modes_ref[b].reshape(rows, LANES)
        ur, ui, gr, gi = [
            jnp.dot(modes, spread_ref[:, k * CC : (k + 1) * CC], preferred_element_type=f32)
            for k in range(4)
        ]
        terms = (
            ur * real - ui * imag,
            ur * imag + ui * real,
            gr * real + gi * imag,
            gi * real - gr * imag,
        )
        mixed = jnp.zeros((rows, LANES), f32)
        for k in range(4):
            mixed += jnp.dot(terms[k].astype(bf16), gather_ref[k], preferred_element_type=f32)
        mixed_ref[b] = mixed.astype(bf16).reshape(owned, ROWS, LANES)
        grad_real += ur * gr + ui * gi
        grad_imag += ur * gi - ui * gr
    for part, gradient in enumerate((grad_real, grad_imag)):
        lanes = slice(part * CC, (part + 1) * CC)
        gradient = gradient.reshape(owned, ROWS, CC)[:, :own]
        new_first = beta_one * first_ref[:, :, lanes] + (1.0 - beta_one) * gradient
        new_second = (
            beta_two * second_ref[:, :, lanes] + (1.0 - beta_two) * gradient * gradient
        )
        corrected = (new_first / (1.0 - beta_one**STEP)) / (
            jnp.sqrt(new_second / (1.0 - beta_two**STEP)) + epsilon
        )
        new_first_ref[:, :, lanes] = new_first
        new_second_ref[:, :, lanes] = new_second
        new_weight_ref[:, :, lanes] = weight_ref[:, :, lanes] - learning_rate * corrected


def mix_and_update(modes, mode_weight, first_moment, second_moment):
    samples, owned = modes.shape[0], modes.shape[1]
    own = mode_weight.shape[1]
    step = min(owned, 4)
    weights = pl.BlockSpec((step, own, 2 * CC), lambda i: (i, 0, 0))
    blocks = pl.BlockSpec((samples, step, ROWS, LANES), lambda i: (0, i, 0, 0))
    like_weight = jax.ShapeDtypeStruct(mode_weight.shape, f32)
    return pl.pallas_call(
        mix_kernel,
        grid=(owned // step,),
        in_specs=[
            blocks,
            weights,
            weights,
            weights,
            pl.BlockSpec((LANES, 4 * CC), lambda i: (0, 0)),
            pl.BlockSpec((4, CC, LANES), lambda i: (0, 0, 0)),
        ],
        out_specs=[blocks, weights, weights, weights],
        out_shape=[jax.ShapeDtypeStruct(modes.shape, bf16), like_weight, like_weight, like_weight],
        scratch_shapes=[pltpu.VMEM((step, ROWS, 2 * CC), f32)],
        compiler_params=pltpu.CompilerParams(vmem_limit_bytes=48 * 2**20),
        name="mix_and_update",
    )(modes, mode_weight, first_moment, second_moment, spread_tables(), gather_tables())


def local(reps, input_field, cotangent, mode_weight, first_moment, second_moment):
    planes = input_field.shape[1]
    cosine, sine = row_tables()
    depth = depth_forward(input_field, cotangent).reshape(planes, NY, C, 8 * KZ)
    slabs = jnp.einsum(
        "qy,xycl->xqcl", cosine, depth[..., : 4 * KZ], preferred_element_type=f32
    ) + jnp.einsum("qy,xycl->xqcl", sine, depth[..., 4 * KZ :], preferred_element_type=f32)
    slabs = slabs.astype(bf16).reshape(planes, KY, C, 2, 2, KZ).transpose(1, 5, 0, 3, 4, 2)
    slabs = slabs.reshape(KY * KZ, planes, LANES)
    columns = lax.all_to_all(slabs, "space", split_axis=0, concat_axis=1, tiled=True)
    modes = grid_modes(columns, reps)
    modes = lax.all_to_all(modes, "rep", split_axis=0, concat_axis=0, tiled=True)
    mixed, new_weight, new_first, new_second = mix_and_update(
        modes, mode_weight, first_moment, second_moment
    )
    mixed = lax.all_to_all(mixed, "rep", split_axis=0, concat_axis=0, tiled=True)
    columns = mode_planes(mixed, reps)
    slabs = lax.all_to_all(columns, "space", split_axis=1, concat_axis=0, tiled=True)
    slabs = slabs.reshape(KY, KZ, planes, 2, 2, C).transpose(2, 0, 5, 3, 4, 1)
    slabs = slabs.reshape(planes, KY, C, 4 * KZ)
    grid_rows = jnp.concatenate(
        [
            jnp.einsum("qy,xqcl->xycl", table, slabs, preferred_element_type=f32).astype(bf16)
            for table in (cosine, sine)
        ],
        axis=-1,
    ).reshape(planes, NY * C, 8 * KZ)
    layer_output, input_gradient = depth_inverse(grid_rows)
    return (layer_output, input_gradient, new_weight, new_first, new_second)


def solution(mesh):
    grids = P("rep", "space", None, None, None)
    weights = P("space", "rep", None)
    return jax.shard_map(
        functools.partial(local, mesh.shape["rep"]),
        mesh=mesh,
        in_specs=(grids, grids, weights, weights, weights),
        out_specs=(grids, grids, weights, weights, weights),
        check_vma=False,
    )
```

```python
import functools
import math

import jax
import jax.numpy as jnp
import numpy as np
from jax import lax
from jax.experimental import pallas as pl
from jax.experimental.pallas import tpu as pltpu
from jax.sharding import PartitionSpec as P

C = 32
NX = 128
NY = 128
NZ = 128
KX = 24
KY = 16
KZ = 16
STEP = 10
CC = C * C
LANES = 4 * C
ROWS = 16

beta_one = 0.9
beta_two = 0.999
learning_rate = 0.001
epsilon = 1e-08
norm_scale = 1.0 / math.sqrt(NX * NY * NZ)

f32 = jnp.float32
bf16 = jnp.bfloat16


def kept_frequency(count, length):
    number = np.arange(count)
    return np.where(number < count // 2, number, length - count + number)


def wave_tables(frequency, length):
    product = frequency[:, None] * np.arange(length)[None, :] % length
    radians = product * (2.0 * math.pi / length)
    return np.cos(radians).astype(np.float32), np.sin(radians).astype(np.float32)


def constant(array):
    return jnp.asarray(np.asarray(array, np.float32), dtype=bf16)


def depth_tables():
    cosine, sine = wave_tables(np.arange(KZ), NZ)
    weighting = np.where(np.arange(KZ) == 0, 1.0, 2.0)[:, None]
    plain = np.concatenate([cosine, -sine], axis=0)
    doubled = np.concatenate([weighting * cosine, -weighting * sine], axis=0)
    return constant(plain), constant(doubled)


def row_tables():
    cosine, sine = wave_tables(kept_frequency(KY, NY), NY)
    return constant(cosine), constant(sine)


def plane_table(reps):
    own = KX // reps
    cosine, sine = wave_tables(kept_frequency(KX, NX), NX)
    tables = np.zeros((2, reps, ROWS, NX), np.float32)
    tables[0, :, :own] = cosine.reshape(reps, own, NX)
    tables[1, :, :own] = sine.reshape(reps, own, NX)
    return tables.reshape(2, reps * ROWS, NX)


def rotation():
    table = np.zeros((LANES, LANES), np.float32)
    for field in range(2):
        for c in range(C):
            real, imag = field * 2 * C + c, field * 2 * C + C + c
            table[imag, real] = 1.0
            table[real, imag] = -1.0
    return constant(table)


def spread_tables():
    table = np.zeros((LANES, 4, CC), np.float32)
    pair = np.arange(CC)
    for part in range(2):
        table[part * C + pair // C, part, pair] = 1.0
        table[2 * C + part * C + pair % C, 2 + part, pair] = 1.0
    return constant(table.reshape(LANES, 4 * CC))


def gather_tables():
    table = np.zeros((4, CC, LANES), np.float32)
    pair = np.arange(CC)
    for part in range(2):
        table[part, pair, part * C + pair % C] = 1.0
        table[2 + part, pair, 2 * C + part * C + pair // C] = 1.0
    return constant(table)


def depth_kernel(field_ref, grad_ref, field_table, grad_table, out_ref):
    out_ref[0] = (
        jnp.dot(field_ref[0], field_table[...], preferred_element_type=f32)
        + jnp.dot(grad_ref[0], grad_table[...], preferred_element_type=f32)
    ).astype(bf16)


def lane_table(table, field):
    real, imag = table[:KZ].T, table[KZ:].T
    own = jnp.concatenate([real, imag], axis=1)
    turned = jnp.concatenate([imag, -real], axis=1)
    none = jnp.zeros_like(own)
    halves = [[half, none] if field == 0 else [none, half] for half in (own, turned)]
    return jnp.concatenate(halves[0] + halves[1], axis=1)


def depth_forward(input_field, cotangent):
    plain, doubled = depth_tables()
    planes = input_field.shape[1]
    rows = NY * C
    block = pl.BlockSpec((1, rows, NZ), lambda i: (i, 0, 0))
    table = pl.BlockSpec((NZ, 8 * KZ), lambda i: (0, 0))
    return pl.pallas_call(
        depth_kernel,
        grid=(planes,),
        in_specs=[block, block, table, table],
        out_specs=pl.BlockSpec((1, rows, 8 * KZ), lambda i: (i, 0, 0)),
        out_shape=jax.ShapeDtypeStruct((planes, rows, 8 * KZ), bf16),
        compiler_params=pltpu.CompilerParams(vmem_limit_bytes=40 * 2**20),
        name="depth_forward",
    )(
        input_field.reshape(planes, rows, NZ),
        cotangent.reshape(planes, rows, NZ),
        lane_table(plain, 0),
        lane_table(doubled, 1),
    )


def grid_kernel(rows_ref, output_table, grad_table, output_ref, grad_ref):
    for ref, table in ((output_ref, output_table), (grad_ref, grad_table)):
        ref[0] = (
            jnp.dot(rows_ref[0], table[...], preferred_element_type=f32) * norm_scale
        ).astype(bf16)


def depth_inverse(rows_in):
    plain, doubled = depth_tables()
    planes, rows = rows_in.shape[0], NY * C
    block = pl.BlockSpec((1, rows, NZ), lambda i: (i, 0, 0))
    table = pl.BlockSpec((4 * KZ, NZ), lambda i: (0, 0))
    outputs = pl.pallas_call(
        grid_kernel,
        grid=(planes,),
        in_specs=[pl.BlockSpec((1, rows, 4 * KZ), lambda i: (i, 0, 0)), table, table],
        out_specs=[block, block],
        out_shape=[jax.ShapeDtypeStruct((planes, rows, NZ), bf16)] * 2,
        compiler_params=pltpu.CompilerParams(vmem_limit_bytes=40 * 2**20),
        name="depth_inverse",
    )(rows_in, lane_table(doubled, 0)[:, : 4 * KZ].T, lane_table(plain, 1)[:, : 4 * KZ].T)
    return [value.reshape(1, planes, NY, C, NZ) for value in outputs]


def modes_kernel(reps, columns_ref, table_ref, turn_ref, out_ref):
    for m in range(columns_ref.shape[0]):
        columns = columns_ref[m]
        turned = jnp.dot(columns, turn_ref[...], preferred_element_type=f32).astype(bf16)
        both = jnp.concatenate([columns, turned], axis=0)
        modes = jnp.dot(table_ref[...], both, preferred_element_type=f32) * norm_scale
        modes = modes.astype(bf16)
        for r in range(reps):
            out_ref[r, m] = modes[r * ROWS : (r + 1) * ROWS]


def grid_modes(columns, reps):
    cosine, sine = plane_table(reps)
    owned = columns.shape[0]
    return pl.pallas_call(
        functools.partial(modes_kernel, reps),
        out_shape=jax.ShapeDtypeStruct((reps, owned, ROWS, LANES), bf16),
        compiler_params=pltpu.CompilerParams(vmem_limit_bytes=40 * 2**20),
        name="grid_modes",
    )(columns, constant(np.concatenate([cosine, sine], axis=1)), rotation())


def planes_kernel(reps, modes_ref, table_ref, turn_ref, out_ref):
    for m in range(out_ref.shape[0]):
        modes = jnp.concatenate([modes_ref[r, m] for r in range(reps)], axis=0)
        turned = jnp.dot(modes, turn_ref[...], preferred_element_type=f32).astype(bf16)
        both = jnp.concatenate([modes, turned], axis=0)
        out_ref[m] = jnp.dot(table_ref[...], both, preferred_element_type=f32).astype(bf16)


def mode_planes(modes, reps):
    cosine, sine = plane_table(reps)
    owned = modes.shape[1]
    return pl.pallas_call(
        functools.partial(planes_kernel, reps),
        out_shape=jax.ShapeDtypeStruct((owned, NX, LANES), bf16),
        compiler_params=pltpu.CompilerParams(vmem_limit_bytes=40 * 2**20),
        name="mode_planes",
    )(modes, constant(np.concatenate([cosine.T, -sine.T], axis=1)), rotation())


def mix_kernel(
    modes_ref, weight_ref, first_ref, second_ref, spread_ref, gather_ref,
    mixed_ref, new_weight_ref, new_first_ref, new_second_ref, padded,
):
    samples, owned = modes_ref.shape[0], modes_ref.shape[1]
    own = weight_ref.shape[1]
    rows = owned * ROWS
    padded[...] = jnp.zeros_like(padded)
    padded[:, :own] = weight_ref[...].astype(bf16).astype(f32)
    weight = padded[...].reshape(rows, 2 * CC)
    real, imag = weight[:, :CC], weight[:, CC:]
    grad_real = jnp.zeros((rows, CC), f32)
    grad_imag = jnp.zeros((rows, CC), f32)
    for b in range(samples):
        modes = modes_ref[b].reshape(rows, LANES)
        ur, ui, gr, gi = [
            jnp.dot(modes, spread_ref[:, k * CC : (k + 1) * CC], preferred_element_type=f32)
            for k in range(4)
        ]
        terms = (
            ur * real - ui * imag,
            ur * imag + ui * real,
            gr * real + gi * imag,
            gi * real - gr * imag,
        )
        mixed = jnp.zeros((rows, LANES), f32)
        for k in range(4):
            mixed += jnp.dot(terms[k].astype(bf16), gather_ref[k], preferred_element_type=f32)
        mixed_ref[b] = mixed.astype(bf16).reshape(owned, ROWS, LANES)
        grad_real += ur * gr + ui * gi
        grad_imag += ur * gi - ui * gr
    for part, gradient in enumerate((grad_real, grad_imag)):
        lanes = slice(part * CC, (part + 1) * CC)
        gradient = gradient.reshape(owned, ROWS, CC)[:, :own]
        new_first = beta_one * first_ref[:, :, lanes] + (1.0 - beta_one) * gradient
        new_second = (
            beta_two * second_ref[:, :, lanes] + (1.0 - beta_two) * gradient * gradient
        )
        corrected = (new_first / (1.0 - beta_one**STEP)) / (
            jnp.sqrt(new_second / (1.0 - beta_two**STEP)) + epsilon
        )
        new_first_ref[:, :, lanes] = new_first
        new_second_ref[:, :, lanes] = new_second
        new_weight_ref[:, :, lanes] = weight_ref[:, :, lanes] - learning_rate * corrected


def mix_and_update(modes, mode_weight, first_moment, second_moment):
    samples, owned = modes.shape[0], modes.shape[1]
    own = mode_weight.shape[1]
    step = min(owned, 4)
    weights = pl.BlockSpec((step, own, 2 * CC), lambda i: (i, 0, 0))
    blocks = pl.BlockSpec((samples, step, ROWS, LANES), lambda i: (0, i, 0, 0))
    like_weight = jax.ShapeDtypeStruct(mode_weight.shape, f32)
    return pl.pallas_call(
        mix_kernel,
        grid=(owned // step,),
        in_specs=[
            blocks,
            weights,
            weights,
            weights,
            pl.BlockSpec((LANES, 4 * CC), lambda i: (0, 0)),
            pl.BlockSpec((4, CC, LANES), lambda i: (0, 0, 0)),
        ],
        out_specs=[blocks, weights, weights, weights],
        out_shape=[jax.ShapeDtypeStruct(modes.shape, bf16), like_weight, like_weight, like_weight],
        scratch_shapes=[pltpu.VMEM((step, ROWS, 2 * CC), f32)],
        compiler_params=pltpu.CompilerParams(vmem_limit_bytes=48 * 2**20),
        name="mix_and_update",
    )(modes, mode_weight, first_moment, second_moment, spread_tables(), gather_tables())


def local(reps, input_field, cotangent, mode_weight, first_moment, second_moment):
    planes = input_field.shape[1]
    cosine, sine = row_tables()
    depth = depth_forward(input_field, cotangent).reshape(planes, NY, C, 8 * KZ)
    slabs = jnp.einsum(
        "qy,xycl->xqcl", cosine, depth[..., : 4 * KZ], preferred_element_type=f32
    ) + jnp.einsum("qy,xycl->xqcl", sine, depth[..., 4 * KZ :], preferred_element_type=f32)
    slabs = slabs.astype(bf16).reshape(planes, KY, C, 2, 2, KZ).transpose(1, 5, 0, 3, 4, 2)
    slabs = slabs.reshape(KY * KZ, planes, LANES)
    columns = lax.all_to_all(slabs, "space", split_axis=0, concat_axis=1, tiled=True)
    modes = grid_modes(columns, reps)
    modes = lax.all_to_all(modes, "rep", split_axis=0, concat_axis=0, tiled=True)
    mixed, new_weight, new_first, new_second = mix_and_update(
        modes, mode_weight, first_moment, second_moment
    )
    mixed = lax.all_to_all(mixed, "rep", split_axis=0, concat_axis=0, tiled=True)
    columns = mode_planes(mixed, reps)
    slabs = lax.all_to_all(columns, "space", split_axis=1, concat_axis=0, tiled=True)
    slabs = slabs.reshape(KY, KZ, planes, 2, 2, C).transpose(2, 0, 5, 3, 4, 1)
    turned = jnp.stack([-slabs[:, :, :, :, 1], slabs[:, :, :, :, 0]], axis=4)
    slabs = jnp.concatenate([slabs, turned], axis=1).reshape(planes, 2 * KY, C, 4 * KZ)
    table = jnp.concatenate([cosine, sine], axis=0)
    grid_rows = jnp.einsum("qy,xqcl->xycl", table, slabs, preferred_element_type=f32)
    grid_rows = grid_rows.astype(bf16).reshape(planes, NY * C, 4 * KZ)
    layer_output, input_gradient = depth_inverse(grid_rows)
    return (layer_output, input_gradient, new_weight, new_first, new_second)


def solution(mesh):
    grids = P("rep", "space", None, None, None)
    weights = P("space", "rep", None)
    return jax.shard_map(
        functools.partial(local, mesh.shape["rep"]),
        mesh=mesh,
        in_specs=(grids, grids, weights, weights, weights),
        out_specs=(grids, grids, weights, weights, weights),
        check_vma=False,
    )
```
